32 devices in a mesh: dp: 4 (over y, core), mp: 8 (over z, x).
Axes of the slice: x: 2, y: 2, z: 4, core: 2. Of those that a mesh axis runs over, the one named last changes fastest.
Arguments:
- table: bfloat16 [8, 2048, 128], P('mp'), may hold values from -6 to 6
- ids: int32 [8192, 8, 2], P('dp', 'mp'), may hold values from 0 to 2047
- counts: int32 [32, 8], P(('dp', 'mp')), may hold values from 1 to 96, 256 in all within a row
- labels: int32 [8192], P(('dp', 'mp')), may hold values from 0 to 4
- request_home: int32 [256], replicated, may hold values from 0 to 255, each once
- user_codes: bfloat16 [256, 1024], P('dp'), may hold values from -6 to 6
- cross_down: bfloat16 [1024, 256], replicated, may hold values from -0.1875 to 0.1875
- cross_up: bfloat16 [256, 1024], replicated, may hold values from -0.375 to 0.375
- cross_bias: float32 [1024], replicated, may hold values from -4 to 4
- tower_weight: bfloat16 [1024, 1024], P('mp'), may hold values from -0.1875 to 0.1875
- tower_bias: float32 [1024], replicated, may hold values from -3 to 3
Outputs:
- scores: float32 [8192], P(('dp', 'mp'))
- pooled_grad: bfloat16 [8192, 8, 128], P('dp', 'mp')
The draws below stay inside these ranges and needn't reach their ends.
Inputs may be any that keep to these rules, and one draw needn't show every extreme that they name: `counts`: each row sums to 256; its largest entry is exactly 96. `request_home`: a permutation of the request slots.
All inputs are finite; a program needn't handle non-finite values.
Results may differ from the reference program's by a relative error of at most 0.0097.
Values may be sent and summed in bfloat16 or wider, within the bound.
A program may use at most 128 MiB of HBM per device.

```python
import math
import jax
import jax.numpy as jnp
import numpy as np
from jax import lax

EMB = 128
FEATURES = 8
D = 1024
R = 256
H = 1024
HOT = 2
TROWS = 2048
ROWS_DEV = 256
SEG_DEV = 8
MOST = 96
CAND = 8192
REQUESTS = 256
N_DP = 4
N_MP = 8


def plant(entries, own_key, least, largest):
    index_at = [jax.random.randint(jax.random.fold_in(own_key, axis), (), 0, length) for axis, length in enumerate(entries.shape)]
    longest = entries.shape.index(max(entries.shape))
    neighbour = index_at[:longest] + [(index_at[longest] + 1) % entries.shape[longest]] + index_at[longest + 1:]
    return entries.at[tuple(index_at)].set(least).at[tuple(neighbour)].set(largest)


def block_levels(rng, shape, pieces, smallest, largest):
    factor_of, own = 1.0, jax.random.fold_in(rng, 6)
    for axis_at, shards_of in pieces:
        heights = jnp.exp(jax.random.uniform(jax.random.fold_in(own, axis_at), (shards_of,), jnp.float32, smallest / len(pieces), largest / len(pieces)))
        factor_of = factor_of * jnp.repeat(heights, shape[axis_at] // shards_of).reshape([-1 if axis == axis_at else 1 for axis in range(len(shape))])
    return factor_of


def split_up(number_of, total, bound, skew):
    loads = [(1 << 20) // math.isqrt(grade ** skew) + 1 for grade in range(2, number_of + 1)]
    rest, given = total - bound - (number_of - 1), [1] * (number_of - 1)
    while rest > 0:
        movable = [i for i in range(number_of - 1) if given[i] < bound]
        whole, budget = sum([loads[i] for i in movable]), rest
        for i in movable:
            addition = min(bound - given[i], max(1, budget * loads[i] // whole), rest)
            given[i] = given[i] + addition
            rest = rest - addition
    return np.array([bound] + given)


def uneven(rng, count, total, most, skew):
    if count == 2:
        one = jax.random.randint(rng, (), max(1, total - most), min(most, total - 1) + 1)
        return jnp.stack([one, total - one])
    tallies = jnp.asarray(split_up(count, total, most, skew), jnp.int32)
    twos = (count - 1) // 2
    source_of, taker = tallies[1:1 + 2 * twos:2], tallies[2:2 + 2 * twos:2]
    margin = jnp.minimum(source_of - 1, most - taker)
    moved = jax.random.randint(jax.random.fold_in(rng, 1), (twos,), 0, 1 << 20) % (margin + 1)
    tallies = tallies.at[1:1 + 2 * twos:2].set(source_of - moved).at[2:2 + 2 * twos:2].set(taker + moved)
    return tallies[jax.random.permutation(jax.random.fold_in(rng, 2), count)]


def centred(stream_key, extent, scale, bound, pieces=(), kind=jnp.bfloat16):
    values = jax.random.normal(stream_key, extent, jnp.float32) * scale
    if len(pieces) > 0:
        values = block_levels(stream_key, extent, pieces, -0.22, 0.18) * values
    return jnp.clip(values, min=-bound, max=bound).astype(kind)


def setup_inputs(seed: int = 0) -> dict:
    seeds = jax.random.split(jax.random.key(seed), 12)
    table = centred(seeds[0], (FEATURES, TROWS, EMB), 1.0, 6.0, ((0, 8),))
    ids = plant(jax.random.randint(seeds[1], (CAND, FEATURES, HOT), 0, TROWS), jax.random.fold_in(seeds[1], 1), 0, TROWS - 1).astype(jnp.int32)
    counts = jax.vmap(lambda own: uneven(own, SEG_DEV, ROWS_DEV, MOST, 2))(jax.random.split(seeds[2], (N_DP * N_MP))).reshape((N_DP * N_MP, SEG_DEV)).astype(jnp.int32)
    labels = plant(jax.random.randint(seeds[3], (CAND,), 0, 5), jax.random.fold_in(seeds[3], 1), 0, 4).astype(jnp.int32)
    request_home = jax.random.permutation(seeds[4], REQUESTS).astype(jnp.int32)
    user_codes = centred(seeds[5], (REQUESTS, H), 1.0, 6.0, ((0, 4),))
    cross_down = centred(seeds[6], (D, R), D ** -0.5, 0.1875)
    cross_up = centred(seeds[7], (R, D), R ** -0.5, 0.375)
    cross_bias = centred(seeds[8], (D,), 1.0, 4.0, (), jnp.float32)
    tower_weight = centred(seeds[9], (D, H), D ** -0.5, 0.1875, ((0, 8),))
    tower_bias = centred(seeds[10], (H,), 0.5, 3.0, (), jnp.float32)
    return dict(table=table, ids=ids, counts=counts, labels=labels, request_home=request_home, user_codes=user_codes, cross_down=cross_down, cross_up=cross_up, cross_bias=cross_bias, tower_weight=tower_weight, tower_bias=tower_bias)


def pool_rows(table, ids):
    feat = table.shape[0]
    picked = table[jnp.arange(feat, dtype=jnp.int32)[None, :, None], ids]
    return lax.optimization_barrier(jnp.sum(picked, axis=2, dtype=jnp.float32)).astype(table.dtype)

def members(counts_row, rows):
    ends = jnp.cumsum(counts_row).astype(jnp.int32)
    starts = ends - counts_row
    place = jnp.arange(rows, dtype=jnp.int32)[:, None]
    return (place >= starts[None, :]) & (place < ends[None, :])

def dot_last(left, right):
    return lax.dot_general(left, right, (((1,), (1,)), ((), ())), preferred_element_type=jnp.float32)

def pair_grad(scores, member, labels):
    gain = jnp.exp2(labels.astype(jnp.float32))
    member_f = member.astype(jnp.float32)
    same = jnp.dot(member_f, member_f.T) > 0.5
    diff = gain[:, None] - gain[None, :]
    gap = scores[None, :] - scores[:, None]
    turn = jnp.where(diff > 0, jax.nn.sigmoid(gap), jax.nn.sigmoid(-gap))
    total = lax.optimization_barrier(jnp.sum(jnp.where(same, diff * turn, 0.0), axis=1))
    seg_gain = lax.optimization_barrier(jnp.sum(jnp.where(member, (gain - 1.0)[:, None], 0.0), axis=0))
    norm = lax.optimization_barrier(jnp.sum(jnp.where(member, seg_gain[None, :], 0.0), axis=1))
    return -total / jnp.maximum(norm, 1.0)

def reference(table, ids, counts, labels, request_home, user_codes, cross_down, cross_up, cross_bias, tower_weight, tower_bias):
    blocks = counts.shape[0]
    seg_count = counts.shape[1]
    rows = labels.shape[0] // blocks
    total_req = request_home.shape[0]
    slot_req = jnp.zeros((total_req,), jnp.int32).at[request_home].set(jnp.arange(total_req, dtype=jnp.int32))
    slot_codes = user_codes[slot_req].reshape(blocks, seg_count, -1)
    ids_b = ids.reshape(blocks, rows, ids.shape[1], ids.shape[2])
    labels_b = labels.reshape(blocks, rows)
    width = user_codes.shape[1]
    scale = 1.0 / jnp.sqrt(jnp.float32(width))

    def one(items):
        ids_blk, counts_row, label_row, user_seg = items
        pooled = pool_rows(table, ids_blk)
        x0 = pooled.reshape(rows, -1)
        member = members(counts_row, rows)
        z = jnp.dot(x0, cross_down, preferred_element_type=jnp.float32).astype(jnp.bfloat16)
        cross = jnp.dot(z, cross_up, preferred_element_type=jnp.float32) + cross_bias
        x1 = (x0 * cross + x0).astype(jnp.bfloat16)
        act = jnp.dot(x1, tower_weight, preferred_element_type=jnp.float32) + tower_bias
        sig = jax.nn.sigmoid(act)
        hidden = (act * sig).astype(jnp.bfloat16)
        pair = dot_last(hidden, user_seg)
        score = lax.optimization_barrier(jnp.sum(jnp.where(member, pair, 0.0), axis=1)) * scale
        dscore = pair_grad(score, member, label_row)
        code = jnp.dot(member.astype(jnp.bfloat16), user_seg, preferred_element_type=jnp.float32)
        slope = sig * (1.0 + act * (1.0 - sig))
        dact = (dscore[:, None] * code * scale * slope).astype(jnp.bfloat16)
        dx1 = dot_last(dact, tower_weight)
        dcross = (dx1 * x0).astype(jnp.bfloat16)
        dz = dot_last(dcross, cross_up).astype(jnp.bfloat16)
        dx0 = dx1 * (1.0 + cross) + dot_last(dz, cross_down)
        return (score, dx0.astype(jnp.bfloat16).reshape(pooled.shape))
    scores, grads = lax.map(one, (ids_b, counts, labels_b, slot_codes))
    return (scores.reshape(-1), grads.reshape(ids.shape[0], ids.shape[1], -1))
```

```python
import functools
import math

import jax
import jax.numpy as jnp
from jax import lax
from jax.experimental import pallas as pl
from jax.experimental.pallas import tpu as pltpu
from jax.sharding import PartitionSpec as P

MESH = pl.DeviceIdType.MESH
F32 = jnp.float32
BF16 = jnp.bfloat16


def nt(left, right):
    return lax.dot_general(left, right, (((1,), (1,)), ((), ())), preferred_element_type=F32)


def kernel(
    grid,
    table_hbm, ids_ref, counts_ref, labels_ref, home_ref, codes_hbm, down_hbm, up_hbm,
    bias_ref, w_hbm, tbias_ref,
    score_ref, out_ref,
    table_v, table_t, codes_v, down, up, w_full, code_parts, code_recv,
    pooled, x0, x1, cross, act, dx1, grads,
    local_sem, w_send, w_recv, y_send, y_recv, c_send, c_recv,
    u_send, u_recv, p_send, p_recv, g_send, g_recv,
):
    n_y, n_z, n_x = grid
    n_mp, n_dp = n_z * n_x, n_y * 2
    rows = x0.shape[0]
    emb = pooled.shape[2]
    width = act.shape[1]
    shard = w_hbm.shape[0]
    part = shard // n_dp
    slots = counts_ref.shape[1]
    depth = n_mp * emb

    dp = lax.axis_index("dp")
    mp = lax.axis_index("mp")
    y, core = dp // 2, lax.rem(dp, 2)
    z, x = mp // n_x, lax.rem(mp, n_x)

    def mp_to(rel):
        a, b = rel // n_x, rel % n_x
        return lax.rem(z + a, n_z) * n_x + lax.rem(x + b, n_x)

    def mp_from(rel):
        a, b = rel // n_x, rel % n_x
        return lax.rem(z + n_z - a, n_z) * n_x + lax.rem(x + n_x - b, n_x)

    def dp_to(c, e):
        return lax.rem(y + c, n_y) * 2 + lax.rem(core + e, 2)

    def dp_from(c, e):
        return lax.rem(y + n_y - c, n_y) * 2 + lax.rem(core + e, 2)

    barrier = pltpu.get_barrier_semaphore()
    for rel in range(1, n_mp):
        pl.semaphore_signal(barrier, inc=1, device_id=(dp, mp_to(rel)), device_id_type=MESH)
    for c in range(n_y):
        for e in range(2):
            if c or e:
                pl.semaphore_signal(barrier, inc=1, device_id=(dp_to(c, e), mp), device_id_type=MESH)

    def w_rows(owner, quarter):
        start = pl.multiple_of(owner * shard + quarter * part, part)
        return w_full.at[pl.ds(start, part)]

    own_w = pltpu.make_async_copy(w_hbm, w_full.at[pl.ds(pl.multiple_of(mp * shard, shard), shard)], local_sem.at[0])
    own_table = pltpu.make_async_copy(table_hbm, table_v, local_sem.at[1])
    own_codes = pltpu.make_async_copy(codes_hbm, codes_v, local_sem.at[2])
    own_down = pltpu.make_async_copy(down_hbm, down, local_sem.at[3])
    own_up = pltpu.make_async_copy(up_hbm, up, local_sem.at[4])
    own_table.start()
    own_w.start()
    own_codes.start()
    own_down.start()
    own_up.start()
    pl.semaphore_wait(barrier, n_mp - 1 + n_dp - 1)

    def remote(src, dst, send, recv, device):
        return pltpu.make_async_remote_copy(
            src_ref=src, dst_ref=dst, send_sem=send, recv_sem=recv, device_id=device, device_id_type=MESH
        )

    sends = []

    def go(copy):
        copy.start()
        sends.append(copy)

    def own_piece():
        return w_hbm.at[pl.ds(pl.multiple_of(dp * part, part), part)]

    for a in range(1, n_z):
        rel = a * n_x
        go(remote(own_piece(), w_rows(mp, dp), w_send.at[rel], w_recv.at[rel], (dp, mp_to(rel))))
    for b in range(1, n_x):
        go(remote(own_piece(), w_rows(mp, dp), w_send.at[b], w_recv.at[b], (dp, mp_to(b))))

    def await_w(rel):
        src = mp_from(rel)
        remote(w_rows(src, dp), w_rows(src, dp), w_send.at[rel], w_recv.at[rel], (dp, src)).wait_recv()

    def spread(rel):
        owner = mp_from(rel)
        for c in range(1, n_y):
            k = c * n_mp + rel
            go(remote(w_rows(owner, dp), w_rows(owner, dp), y_send.at[k], y_recv.at[k], (dp_to(c, 0), mp)))
        go(remote(w_rows(owner, dp), w_rows(owner, dp), c_send.at[rel], c_recv.at[rel], (dp_to(0, 1), mp)))

    def relay_z(a):
        rel = a * n_x
        await_w(rel)
        owner = mp_from(rel)
        for b in range(1, n_x):
            go(remote(w_rows(owner, dp), w_rows(owner, dp), w_send.at[rel + b], w_recv.at[rel + b], (dp, mp_to(b))))
        spread(rel)

    def relay_x(rel):
        await_w(rel)
        spread(rel)

    def relay_y(rel):
        owner = mp_from(rel)
        for c in range(1, n_y):
            k = c * n_mp + rel
            quarter = dp_from(c, 0)
            ref = w_rows(owner, quarter)
            remote(ref, ref, y_send.at[k], y_recv.at[k], (quarter, mp)).wait_recv()
            go(remote(ref, ref, c_send.at[k], c_recv.at[k], (dp_to(0, 1), mp)))

    own_codes.wait()
    users = codes_v.shape[0]
    home = home_ref[...]
    homes = home[0:1, :]
    for k in range(1, n_dp):
        homes = jnp.where(dp == k, home[k:k + 1, :], homes)

    def code_part(target):
        base = (target * n_mp + mp) * slots
        wanted = base + lax.broadcasted_iota(jnp.int32, (slots, users), 0)
        pick = (homes == wanted).astype(F32).astype(BF16)
        return jnp.dot(pick, codes_v[...], preferred_element_type=F32)

    for c in range(n_y):
        for e in range(2):
            i = c * 2 + e
            code_parts[i] = code_part(dp_to(c, e))
            if i:
                go(remote(code_parts.at[i], code_recv.at[i], u_send.at[i], u_recv.at[i], (dp_to(c, e), mp)))

    own_table.wait()
    t_rows = table_v.shape[0]
    for i in range(t_rows // emb):
        block = table_v[pl.ds(i * emb, emb), :].astype(F32)
        table_t[:, pl.ds(i * emb, emb)] = block.T.astype(BF16)

    chunk = 512 if t_rows % 512 == 0 else t_rows

    def pool(target):
        picked = ids_ref[:, pl.ds(pl.multiple_of(target * rows, rows), rows)]
        total = jnp.zeros((emb, rows), F32)
        for i in range(t_rows // chunk):
            lanes = lax.broadcasted_iota(jnp.int32, (chunk, rows), 0) + i * chunk
            tally = jnp.zeros((chunk, rows), F32)
            for which in range(picked.shape[0]):
                tally = tally + jnp.where(lanes == picked[which:which + 1, :], 1.0, 0.0)
            total = total + jnp.dot(
                table_t[:, pl.ds(i * chunk, chunk)], tally.astype(BF16), preferred_element_type=F32
            )
        return total.T.astype(BF16)

    def columns(f):
        return pl.ds(pl.multiple_of(f * emb, emb), emb)

    def pool_send(low, high):
        def body(i, carry):
            rel = n_mp - 1 - i
            target = mp_to(rel)
            pooled[rel] = pool(target)
            remote(pooled.at[rel], x0.at[:, columns(mp)], p_send.at[rel], p_recv.at[rel], (dp, target)).start()
            return carry

        lax.fori_loop(low, high, body, 0)

    cut_a = (n_mp - 1) * 2 // 7
    cut_b = (n_mp - 1) * 4 // 7
    pool_send(0, cut_a)
    for a in range(1, n_z):
        relay_z(a)
    pool_send(cut_a, cut_b)
    for b in range(1, n_x):
        for a in range(n_z):
            relay_x(a * n_x + b)
    pool_send(cut_b, n_mp - 1)
    x0[:, columns(mp)] = pool(mp)

    place = lax.broadcasted_iota(jnp.int32, (1, rows), 1)
    place_c = lax.broadcasted_iota(jnp.int32, (rows, 1), 0)
    seg = jnp.zeros((1, rows), jnp.int32)
    seg_c = jnp.zeros((rows, 1), jnp.int32)
    end = jnp.int32(0)
    for q in range(slots - 1):
        end = end + counts_ref[0, q]
        seg = seg + jnp.where(place >= end, 1, 0)
        seg_c = seg_c + jnp.where(place_c >= end, 1, 0)
    eye = place == place_c
    same = seg == seg_c
    labels = labels_ref[...]
    gain = jnp.ones((1, rows), F32)
    for level, step in ((1, 1.0), (2, 2.0), (3, 4.0), (4, 8.0)):
        gain = gain + jnp.where(labels >= level, step, 0.0)
    gain_c = jnp.sum(jnp.where(eye, gain, 0.0), axis=1, keepdims=True)
    norm = jnp.sum(jnp.where(same, gain - 1.0, 0.0), axis=1, keepdims=True)
    member = (seg_c == lax.broadcasted_iota(jnp.int32, (rows, slots), 1)).astype(F32).astype(BF16)

    for rel in sorted(range(1, n_mp), key=lambda r: (r % n_x > 0, r)):
        relay_y(rel)

    user_seg = code_parts[0]
    for i in range(1, n_dp):
        src = dp_from(i // 2, i % 2)
        remote(code_parts.at[i], code_recv.at[i], u_send.at[i], u_recv.at[i], (src, mp)).wait_recv()
        user_seg = user_seg + code_recv[i]
    user_seg = user_seg.astype(BF16)

    own_down.wait()
    own_up.wait()
    for rel in range(1, n_mp):
        src = mp_from(rel)
        remote(pooled.at[rel], x0.at[:, columns(src)], p_send.at[rel], p_recv.at[rel], (dp, src)).wait_recv()
    low = jnp.dot(x0[...], down[...], preferred_element_type=F32).astype(BF16)
    tile = 256

    def over(extent, body):
        step = tile if extent % tile == 0 else extent

        def run(i, carry):
            body(pl.ds(pl.multiple_of(i * step, step), step))
            return carry

        lax.fori_loop(0, extent // step, run, 0)

    def forward_cross(cols):
        lift = jnp.dot(low, up[:, cols], preferred_element_type=F32) + bias_ref[:, cols]
        own = x0[:, cols].astype(F32)
        cross[:, cols] = lift
        x1[:, cols] = (own * lift + own).astype(BF16)

    over(depth, forward_cross)

    own_w.wait()
    for rel in range(1, n_mp):
        owner = mp_from(rel)
        for c in range(n_y):
            k = c * n_mp + rel
            quarter = dp_from(c, 1)
            ref = w_rows(owner, quarter)
            remote(ref, ref, c_send.at[k], c_recv.at[k], (dp_to(0, 1), mp)).wait_recv()

    def forward_tower(cols):
        act[:, cols] = jnp.dot(x1[...], w_full[:, cols], preferred_element_type=F32) + tbias_ref[:, cols]

    over(width, forward_tower)
    scale = 1.0 / math.sqrt(width)
    value = act[...]
    sig = jax.nn.sigmoid(value)
    hidden = (value * sig).astype(BF16)
    code = jnp.dot(member, user_seg, preferred_element_type=F32)
    score_c = jnp.sum(hidden.astype(F32) * code, axis=1, keepdims=True) * scale
    score = jnp.sum(jnp.where(eye, score_c, 0.0), axis=0, keepdims=True)
    score_ref[...] = score

    diff = gain_c - gain
    gap = score - score_c
    turn = jax.nn.sigmoid(jnp.where(diff > 0, gap, -gap))
    total = jnp.sum(jnp.where(same, diff * turn, 0.0), axis=1, keepdims=True)
    dscore = -total / jnp.maximum(norm, 1.0)
    slope = sig * (1.0 + value * (1.0 - sig))
    dact = ((dscore * scale) * code * slope).astype(BF16)

    def backward_tower(cols):
        dx1[:, cols] = nt(dact, w_full[cols, :])

    over(depth, backward_tower)
    dcross = (dx1[...] * x0[...].astype(F32)).astype(BF16)
    dlow = nt(dcross, up[...]).astype(BF16)

    def grad(cols):
        flow = dx1[:, cols] * (1.0 + cross[:, cols]) + nt(dlow, down[cols, :])
        return flow.astype(BF16)

    def mine(f):
        return pl.ds(pl.multiple_of(f * rows, rows), rows)

    def grad_send(i, carry):
        rel = n_mp - 1 - i
        target = mp_to(rel)
        grads[rel] = grad(columns(target))
        remote(grads.at[rel], out_ref.at[mine(mp)], g_send.at[rel], g_recv.at[rel], (dp, target)).start()
        return carry

    lax.fori_loop(0, n_mp - 1, grad_send, 0)
    out_ref[mine(mp), :] = grad(columns(mp))

    for copy in sends:
        copy.wait_send()
    for rel in range(1, n_mp):
        target = mp_to(rel)
        src = mp_from(rel)
        remote(pooled.at[rel], x0.at[:, columns(mp)], p_send.at[rel], p_recv.at[rel], (dp, target)).wait_send()
        remote(grads.at[rel], out_ref.at[mine(mp)], g_send.at[rel], g_recv.at[rel], (dp, target)).wait_send()
        remote(grads.at[rel], out_ref.at[mine(src)], g_send.at[rel], g_recv.at[rel], (dp, src)).wait_recv()


def local(n_dp, n_mp, table, ids, counts, labels, request_home, user_codes, cross_down, cross_up, cross_bias,
          tower_weight, tower_bias):
    n_x = max(d for d in range(1, math.isqrt(n_mp) + 1) if n_mp % d == 0)
    grid = (n_dp // 2, n_mp // n_x, n_x)
    rows = labels.shape[0]
    _, t_rows, emb = table.shape
    users, width = user_codes.shape
    depth, rank = cross_down.shape
    slots = counts.shape[1]
    everyone = rows * n_mp
    dma = pltpu.SemaphoreType.DMA
    hbm = pl.BlockSpec(memory_space=pl.ANY)
    vmem = pl.BlockSpec(memory_space=pltpu.VMEM)
    smem = pl.BlockSpec(memory_space=pltpu.SMEM)
    score, out = pl.pallas_call(
        functools.partial(kernel, grid),
        out_shape=(
            jax.ShapeDtypeStruct((1, rows), F32),
            jax.ShapeDtypeStruct((everyone, emb), BF16),
        ),
        in_specs=[hbm, vmem, smem, vmem, vmem, hbm, hbm, hbm, vmem, hbm, vmem],
        out_specs=(vmem, vmem),
        scratch_shapes=[
            pltpu.VMEM((t_rows, emb), BF16),
            pltpu.VMEM((emb, t_rows), BF16),
            pltpu.VMEM((users, width), BF16),
            pltpu.VMEM((depth, rank), BF16),
            pltpu.VMEM((rank, depth), BF16),
            pltpu.VMEM((depth, width), BF16),
            pltpu.VMEM((n_dp, slots, width), F32),
            pltpu.VMEM((n_dp, slots, width), F32),
            pltpu.VMEM((n_mp, rows, emb), BF16),
            pltpu.VMEM((rows, depth), BF16),
            pltpu.VMEM((rows, depth), BF16),
            pltpu.VMEM((rows, depth), F32),
            pltpu.VMEM((rows, width), F32),
            pltpu.VMEM((rows, depth), F32),
            pltpu.VMEM((n_mp, rows, emb), BF16),
            dma((5,)),
            dma((n_mp,)),
            dma((n_mp,)),
            dma((grid[0] * n_mp,)),
            dma((grid[0] * n_mp,)),
            dma((grid[0] * n_mp,)),
            dma((grid[0] * n_mp,)),
            dma((n_dp,)),
            dma((n_dp,)),
            dma((n_mp,)),
            dma((n_mp,)),
            dma((n_mp,)),
            dma((n_mp,)),
        ],
        compiler_params=pltpu.CompilerParams(
            collective_id=0, has_side_effects=True, vmem_limit_bytes=48 * 1024 * 1024
        ),
    )(
        table[0], ids[:, 0, :].T, counts, labels[None, :], request_home.reshape(n_dp, users), user_codes,
        cross_down, cross_up, cross_bias[None, :], tower_weight, tower_bias[None, :],
    )
    return score[0], out[:, None, :]


def solution(mesh):
    in_specs = (
        P("mp", None, None),
        P("dp", "mp", None),
        P(("dp", "mp"), None),
        P(("dp", "mp")),
        P(),
        P("dp", None),
        P(),
        P(),
        P(),
        P("mp", None),
        P(),
    )
    out_specs = (P(("dp", "mp")), P("dp", "mp", None))
    body = functools.partial(local, mesh.shape["dp"], mesh.shape["mp"])
    return jax.shard_map(body, mesh=mesh, in_specs=in_specs, out_specs=out_specs, check_vma=False)
```

```python
import functools
import math

import jax
import jax.numpy as jnp
from jax import lax
from jax.experimental import pallas as pl
from jax.experimental.pallas import tpu as pltpu
from jax.sharding import PartitionSpec as P

MESH = pl.DeviceIdType.MESH
F32 = jnp.float32
BF16 = jnp.bfloat16


def nt(left, right):
    return lax.dot_general(left, right, (((1,), (1,)), ((), ())), preferred_element_type=F32)


def kernel(
    grid,
    table_hbm, ids_ref, counts_ref, labels_ref, home_ref, codes_hbm, down_hbm, up_hbm,
    bias_ref, w_hbm, tbias_ref,
    score_ref, out_ref,
    table_v, table_t, codes_v, down, up, w_full, code_parts, code_recv,
    pooled, x0, x1, cross, act, dx1, grads,
    local_sem, w_send, w_recv, y_send, y_recv, c_send, c_recv,
    u_send, u_recv, p_send, p_recv, g_send, g_recv,
):
    n_y, n_z, n_x = grid
    n_mp, n_dp = n_z * n_x, n_y * 2
    rows = x0.shape[0]
    emb = pooled.shape[2]
    width = act.shape[1]
    shard = w_hbm.shape[0]
    part = shard // n_dp
    slots = counts_ref.shape[1]
    depth = n_mp * emb

    dp = lax.axis_index("dp")
    mp = lax.axis_index("mp")
    y, core = dp // 2, lax.rem(dp, 2)
    z, x = mp // n_x, lax.rem(mp, n_x)

    def mp_to(rel):
        a, b = rel // n_x, rel % n_x
        return lax.rem(z + a, n_z) * n_x + lax.rem(x + b, n_x)

    def mp_from(rel):
        a, b = rel // n_x, rel % n_x
        return lax.rem(z + n_z - a, n_z) * n_x + lax.rem(x + n_x - b, n_x)

    def dp_to(c, e):
        return lax.rem(y + c, n_y) * 2 + lax.rem(core + e, 2)

    def dp_from(c, e):
        return lax.rem(y + n_y - c, n_y) * 2 + lax.rem(core + e, 2)

    barrier = pltpu.get_barrier_semaphore()
    for rel in range(1, n_mp):
        pl.semaphore_signal(barrier, inc=1, device_id=(dp, mp_to(rel)), device_id_type=MESH)
    for c in range(n_y):
        for e in range(2):
            if c or e:
                pl.semaphore_signal(barrier, inc=1, device_id=(dp_to(c, e), mp), device_id_type=MESH)

    def w_rows(owner, quarter):
        start = pl.multiple_of(owner * shard + quarter * part, part)
        return w_full.at[pl.ds(start, part)]

    own_w = pltpu.make_async_copy(w_hbm, w_full.at[pl.ds(pl.multiple_of(mp * shard, shard), shard)], local_sem.at[0])
    own_table = pltpu.make_async_copy(table_hbm, table_v, local_sem.at[1])
    own_codes = pltpu.make_async_copy(codes_hbm, codes_v, local_sem.at[2])
    own_down = pltpu.make_async_copy(down_hbm, down, local_sem.at[3])
    own_up = pltpu.make_async_copy(up_hbm, up, local_sem.at[4])
    own_table.start()
    own_w.start()
    own_codes.start()
    own_down.start()
    own_up.start()
    pl.semaphore_wait(barrier, n_mp - 1 + n_dp - 1)

    def remote(src, dst, send, recv, device):
        return pltpu.make_async_remote_copy(
            src_ref=src, dst_ref=dst, send_sem=send, recv_sem=recv, device_id=device, device_id_type=MESH
        )

    sends = []

    def go(copy):
        copy.start()
        sends.append(copy)

    def own_piece():
        return w_hbm.at[pl.ds(pl.multiple_of(dp * part, part), part)]

    for a in range(1, n_z):
        rel = a * n_x
        go(remote(own_piece(), w_rows(mp, dp), w_send.at[rel], w_recv.at[rel], (dp, mp_to(rel))))
    for b in range(1, n_x):
        go(remote(own_piece(), w_rows(mp, dp), w_send.at[b], w_recv.at[b], (dp, mp_to(b))))

    def await_w(rel):
        src = mp_from(rel)
        remote(w_rows(src, dp), w_rows(src, dp), w_send.at[rel], w_recv.at[rel], (dp, src)).wait_recv()

    def spread(rel):
        owner = mp_from(rel)
        for c in range(1, n_y):
            k = c * n_mp + rel
            go(remote(w_rows(owner, dp), w_rows(owner, dp), y_send.at[k], y_recv.at[k], (dp_to(c, 0), mp)))
        go(remote(w_rows(owner, dp), w_rows(owner, dp), c_send.at[rel], c_recv.at[rel], (dp_to(0, 1), mp)))

    def relay_z(a):
        rel = a * n_x
        await_w(rel)
        owner = mp_from(rel)
        for b in range(1, n_x):
            go(remote(w_rows(owner, dp), w_rows(owner, dp), w_send.at[rel + b], w_recv.at[rel + b], (dp, mp_to(b))))
        spread(rel)

    def relay_x(rel):
        await_w(rel)
        spread(rel)

    def relay_y(rel):
        owner = mp_from(rel)
        for c in range(1, n_y):
            k = c * n_mp + rel
            quarter = dp_from(c, 0)
            ref = w_rows(owner, quarter)
            remote(ref, ref, y_send.at[k], y_recv.at[k], (quarter, mp)).wait_recv()
            go(remote(ref, ref, c_send.at[k], c_recv.at[k], (dp_to(0, 1), mp)))

    own_codes.wait()
    users = codes_v.shape[0]
    home = home_ref[...]
    homes = home[:, :users]
    for k in range(1, n_dp):
        homes = jnp.where(dp == k, home[:, k * users:(k + 1) * users], homes)

    def code_part(target):
        base = (target * n_mp + mp) * slots
        wanted = base + lax.broadcasted_iota(jnp.int32, (slots, users), 0)
        pick = (homes == wanted).astype(F32).astype(BF16)
        return jnp.dot(pick, codes_v[...], preferred_element_type=F32)

    for c in range(n_y):
        for e in range(2):
            i = c * 2 + e
            code_parts[i] = code_part(dp_to(c, e))
            if i:
                go(remote(code_parts.at[i], code_recv.at[i], u_send.at[i], u_recv.at[i], (dp_to(c, e), mp)))

    own_table.wait()
    t_rows = table_v.shape[0]
    for i in range(t_rows // emb):
        block = table_v[pl.ds(i * emb, emb), :].astype(F32)
        table_t[:, pl.ds(i * emb, emb)] = block.T.astype(BF16)

    chunk = 512 if t_rows % 512 == 0 else t_rows

    def pool(target):
        picked = ids_ref[:, pl.ds(pl.multiple_of(target * rows, rows), rows)]
        total = jnp.zeros((emb, rows), F32)
        for i in range(t_rows // chunk):
            lanes = lax.broadcasted_iota(jnp.int32, (chunk, rows), 0) + i * chunk
            tally = jnp.zeros((chunk, rows), F32)
            for which in range(picked.shape[0]):
                tally = tally + jnp.where(lanes == picked[which:which + 1, :], 1.0, 0.0)
            total = total + jnp.dot(
                table_t[:, pl.ds(i * chunk, chunk)], tally.astype(BF16), preferred_element_type=F32
            )
        return total.T.astype(BF16)

    def columns(f):
        return pl.ds(pl.multiple_of(f * emb, emb), emb)

    def pool_send(low, high):
        def body(i, carry):
            rel = n_mp - 1 - i
            target = mp_to(rel)
            pooled[rel] = pool(target)
            remote(pooled.at[rel], x0.at[:, columns(mp)], p_send.at[rel], p_recv.at[rel], (dp, target)).start()
            return carry

        lax.fori_loop(low, high, body, 0)

    cut_a = (n_mp - 1) * 2 // 7
    cut_b = (n_mp - 1) * 4 // 7
    pool_send(0, cut_a)
    for a in range(1, n_z):
        relay_z(a)
    pool_send(cut_a, cut_b)
    for b in range(1, n_x):
        for a in range(n_z):
            relay_x(a * n_x + b)
    pool_send(cut_b, n_mp - 1)
    x0[:, columns(mp)] = pool(mp)

    place = lax.broadcasted_iota(jnp.int32, (1, rows), 1)
    place_c = lax.broadcasted_iota(jnp.int32, (rows, 1), 0)
    seg = jnp.zeros((1, rows), jnp.int32)
    seg_c = jnp.zeros((rows, 1), jnp.int32)
    end = jnp.int32(0)
    for q in range(slots - 1):
        end = end + counts_ref[0, q]
        seg = seg + jnp.where(place >= end, 1, 0)
        seg_c = seg_c + jnp.where(place_c >= end, 1, 0)
    eye = place == place_c
    same = seg == seg_c
    labels = labels_ref[...]
    gain = jnp.ones((1, rows), F32)
    for level, step in ((1, 1.0), (2, 2.0), (3, 4.0), (4, 8.0)):
        gain = gain + jnp.where(labels >= level, step, 0.0)
    gain_c = jnp.sum(jnp.where(eye, gain, 0.0), axis=1, keepdims=True)
    norm = jnp.sum(jnp.where(same, gain - 1.0, 0.0), axis=1, keepdims=True)
    member = (seg_c == lax.broadcasted_iota(jnp.int32, (rows, slots), 1)).astype(F32).astype(BF16)

    for rel in sorted(range(1, n_mp), key=lambda r: (r % n_x > 0, r)):
        relay_y(rel)

    user_seg = code_parts[0]
    for i in range(1, n_dp):
        src = dp_from(i // 2, i % 2)
        remote(code_parts.at[i], code_recv.at[i], u_send.at[i], u_recv.at[i], (src, mp)).wait_recv()
        user_seg = user_seg + code_recv[i]
    user_seg = user_seg.astype(BF16)

    own_down.wait()
    own_up.wait()
    for rel in range(1, n_mp):
        src = mp_from(rel)
        remote(pooled.at[rel], x0.at[:, columns(src)], p_send.at[rel], p_recv.at[rel], (dp, src)).wait_recv()
    low = jnp.dot(x0[...], down[...], preferred_element_type=F32).astype(BF16)
    tile = 256

    def over(extent, body):
        step = tile if extent % tile == 0 else extent

        def run(i, carry):
            body(pl.ds(pl.multiple_of(i * step, step), step))
            return carry

        lax.fori_loop(0, extent // step, run, 0)

    def forward_cross(cols):
        lift = jnp.dot(low, up[:, cols], preferred_element_type=F32) + bias_ref[:, cols]
        own = x0[:, cols].astype(F32)
        cross[:, cols] = lift
        x1[:, cols] = (own * lift + own).astype(BF16)

    over(depth, forward_cross)

    own_w.wait()
    for rel in range(1, n_mp):
        owner = mp_from(rel)
        for c in range(n_y):
            k = c * n_mp + rel
            quarter = dp_from(c, 1)
            ref = w_rows(owner, quarter)
            remote(ref, ref, c_send.at[k], c_recv.at[k], (dp_to(0, 1), mp)).wait_recv()

    def forward_tower(cols):
        act[:, cols] = jnp.dot(x1[...], w_full[:, cols], preferred_element_type=F32) + tbias_ref[:, cols]

    over(width, forward_tower)
    scale = 1.0 / math.sqrt(width)
    value = act[...]
    sig = jax.nn.sigmoid(value)
    hidden = (value * sig).astype(BF16)
    code = jnp.dot(member, user_seg, preferred_element_type=F32)
    score_c = jnp.sum(hidden.astype(F32) * code, axis=1, keepdims=True) * scale
    score = jnp.sum(jnp.where(eye, score_c, 0.0), axis=0, keepdims=True)
    score_ref[...] = score

    diff = gain_c - gain
    gap = score - score_c
    turn = jax.nn.sigmoid(jnp.where(diff > 0, gap, -gap))
    total = jnp.sum(jnp.where(same, diff * turn, 0.0), axis=1, keepdims=True)
    dscore = -total / jnp.maximum(norm, 1.0)
    slope = sig * (1.0 + value * (1.0 - sig))
    dact = ((dscore * scale) * code * slope).astype(BF16)

    def backward_tower(cols):
        dx1[:, cols] = nt(dact, w_full[cols, :])

    over(depth, backward_tower)
    dcross = (dx1[...] * x0[...].astype(F32)).astype(BF16)
    dlow = nt(dcross, up[...]).astype(BF16)

    def grad(cols):
        flow = dx1[:, cols] * (1.0 + cross[:, cols]) + nt(dlow, down[cols, :])
        return flow.astype(BF16)

    def mine(f):
        return pl.ds(pl.multiple_of(f * rows, rows), rows)

    def grad_send(i, carry):
        rel = n_mp - 1 - i
        target = mp_to(rel)
        grads[rel] = grad(columns(target))
        remote(grads.at[rel], out_ref.at[mine(mp)], g_send.at[rel], g_recv.at[rel], (dp, target)).start()
        return carry

    lax.fori_loop(0, n_mp - 1, grad_send, 0)
    out_ref[mine(mp), :] = grad(columns(mp))

    for copy in sends:
        copy.wait_send()
    for rel in range(1, n_mp):
        target = mp_to(rel)
        src = mp_from(rel)
        remote(pooled.at[rel], x0.at[:, columns(mp)], p_send.at[rel], p_recv.at[rel], (dp, target)).wait_send()
        remote(grads.at[rel], out_ref.at[mine(mp)], g_send.at[rel], g_recv.at[rel], (dp, target)).wait_send()
        remote(grads.at[rel], out_ref.at[mine(src)], g_send.at[rel], g_recv.at[rel], (dp, src)).wait_recv()


def local(n_dp, n_mp, table, ids, counts, labels, request_home, user_codes, cross_down, cross_up, cross_bias,
          tower_weight, tower_bias):
    n_x = max(d for d in range(1, math.isqrt(n_mp) + 1) if n_mp % d == 0)
    grid = (n_dp // 2, n_mp // n_x, n_x)
    rows = labels.shape[0]
    _, t_rows, emb = table.shape
    users, width = user_codes.shape
    depth, rank = cross_down.shape
    slots = counts.shape[1]
    everyone = rows * n_mp
    dma = pltpu.SemaphoreType.DMA
    hbm = pl.BlockSpec(memory_space=pltpu.HBM)
    vmem = pl.BlockSpec(memory_space=pltpu.VMEM)
    smem = pl.BlockSpec(memory_space=pltpu.SMEM)
    score, out = pl.pallas_call(
        functools.partial(kernel, grid),
        out_shape=(
            jax.ShapeDtypeStruct((1, rows), F32),
            jax.ShapeDtypeStruct((everyone, emb), BF16),
        ),
        in_specs=[hbm, vmem, smem, vmem, vmem, hbm, hbm, hbm, vmem, hbm, vmem],
        out_specs=(vmem, vmem),
        scratch_shapes=[
            pltpu.VMEM((t_rows, emb), BF16),
            pltpu.VMEM((emb, t_rows), BF16),
            pltpu.VMEM((users, width), BF16),
            pltpu.VMEM((depth, rank), BF16),
            pltpu.VMEM((rank, depth), BF16),
            pltpu.VMEM((depth, width), BF16),
            pltpu.VMEM((n_dp, slots, width), F32),
            pltpu.VMEM((n_dp, slots, width), F32),
            pltpu.VMEM((n_mp, rows, emb), BF16),
            pltpu.VMEM((rows, depth), BF16),
            pltpu.VMEM((rows, depth), BF16),
            pltpu.VMEM((rows, depth), F32),
            pltpu.VMEM((rows, width), F32),
            pltpu.VMEM((rows, depth), F32),
            pltpu.VMEM((n_mp, rows, emb), BF16),
            dma((5,)),
            dma((n_mp,)),
            dma((n_mp,)),
            dma((grid[0] * n_mp,)),
            dma((grid[0] * n_mp,)),
            dma((grid[0] * n_mp,)),
            dma((grid[0] * n_mp,)),
            dma((n_dp,)),
            dma((n_dp,)),
            dma((n_mp,)),
            dma((n_mp,)),
            dma((n_mp,)),
            dma((n_mp,)),
        ],
        compiler_params=pltpu.CompilerParams(
            collective_id=0, has_side_effects=True, vmem_limit_bytes=56 * 1024 * 1024
        ),
    )(
        table[0], ids[:, 0, :].T, counts, labels[None, :], request_home[None, :], user_codes,
        cross_down, cross_up, cross_bias[None, :], tower_weight, tower_bias[None, :],
    )
    return score[0], out[:, None, :]


def solution(mesh):
    in_specs = (
        P("mp", None, None),
        P("dp", "mp", None),
        P(("dp", "mp"), None),
        P(("dp", "mp")),
        P(),
        P("dp", None),
        P(),
        P(),
        P(),
        P("mp", None),
        P(),
    )
    out_specs = (P(("dp", "mp")), P("dp", "mp", None))
    body = functools.partial(local, mesh.shape["dp"], mesh.shape["mp"])
    return jax.shard_map(body, mesh=mesh, in_specs=in_specs, out_specs=out_specs, check_vma=False)
```

```python
import functools
import math

import jax
import jax.numpy as jnp
from jax import lax
from jax.experimental import pallas as pl
from jax.experimental.pallas import tpu as pltpu
from jax.sharding import PartitionSpec as P

MESH = pl.DeviceIdType.MESH
F32 = jnp.float32
BF16 = jnp.bfloat16


def nt(left, right):
    return lax.dot_general(left, right, (((1,), (1,)), ((), ())), preferred_element_type=F32)


def kernel(
    grid,
    table_hbm, ids_ref, counts_ref, labels_ref, home_ref, codes_hbm, down_hbm, up_hbm,
    bias_ref, w_hbm, tbias_ref,
    score_ref, out_ref,
    table_v, table_t, codes_v, down, up, w_full, code_parts, code_recv,
    pooled, x0, x1, cross, act, dx1, grads,
    local_sem, w_send, w_recv, y_send, y_recv, c_send, c_recv,
    u_send, u_recv, p_send, p_recv, g_send, g_recv,
):
    n_y, n_z, n_x = grid
    n_mp, n_dp = n_z * n_x, n_y * 2
    rows = x0.shape[0]
    emb = pooled.shape[2]
    width = act.shape[1]
    shard = w_hbm.shape[0]
    part = shard // n_dp
    slots = counts_ref.shape[1]
    depth = n_mp * emb

    dp = lax.axis_index("dp")
    mp = lax.axis_index("mp")
    y, core = dp // 2, lax.rem(dp, 2)
    z, x = mp // n_x, lax.rem(mp, n_x)

    def mp_to(rel):
        a, b = rel // n_x, rel % n_x
        return lax.rem(z + a, n_z) * n_x + lax.rem(x + b, n_x)

    def mp_from(rel):
        a, b = rel // n_x, rel % n_x
        return lax.rem(z + n_z - a, n_z) * n_x + lax.rem(x + n_x - b, n_x)

    def dp_to(c, e):
        return lax.rem(y + c, n_y) * 2 + lax.rem(core + e, 2)

    def dp_from(c, e):
        return lax.rem(y + n_y - c, n_y) * 2 + lax.rem(core + e, 2)

    barrier = pltpu.get_barrier_semaphore()
    for rel in range(1, n_mp):
        pl.semaphore_signal(barrier, inc=1, device_id=(dp, mp_to(rel)), device_id_type=MESH)
    for c in range(n_y):
        for e in range(2):
            if c or e:
                pl.semaphore_signal(barrier, inc=1, device_id=(dp_to(c, e), mp), device_id_type=MESH)

    def w_rows(owner, quarter):
        start = pl.multiple_of(owner * shard + quarter * part, part)
        return w_full.at[pl.ds(start, part)]

    own_w = pltpu.make_async_copy(w_hbm, w_full.at[pl.ds(pl.multiple_of(mp * shard, shard), shard)], local_sem.at[0])
    own_table = pltpu.make_async_copy(table_hbm, table_v, local_sem.at[1])
    own_codes = pltpu.make_async_copy(codes_hbm, codes_v, local_sem.at[2])
    own_down = pltpu.make_async_copy(down_hbm, down, local_sem.at[3])
    own_up = pltpu.make_async_copy(up_hbm, up, local_sem.at[4])
    own_table.start()
    own_w.start()
    own_codes.start()
    own_down.start()
    own_up.start()
    pl.semaphore_wait(barrier, n_mp - 1 + n_dp - 1)

    def remote(src, dst, send, recv, device):
        return pltpu.make_async_remote_copy(
            src_ref=src, dst_ref=dst, send_sem=send, recv_sem=recv, device_id=device, device_id_type=MESH
        )

    sends = []

    def go(copy):
        copy.start()
        sends.append(copy)

    def own_piece():
        return w_hbm.at[pl.ds(pl.multiple_of(dp * part, part), part)]

    for a in range(1, n_z):
        rel = a * n_x
        go(remote(own_piece(), w_rows(mp, dp), w_send.at[rel], w_recv.at[rel], (dp, mp_to(rel))))
    for b in range(1, n_x):
        go(remote(own_piece(), w_rows(mp, dp), w_send.at[b], w_recv.at[b], (dp, mp_to(b))))

    def await_w(rel):
        src = mp_from(rel)
        remote(w_rows(src, dp), w_rows(src, dp), w_send.at[rel], w_recv.at[rel], (dp, src)).wait_recv()

    def spread(rel):
        owner = mp_from(rel)
        for c in range(1, n_y):
            k = c * n_mp + rel
            go(remote(w_rows(owner, dp), w_rows(owner, dp), y_send.at[k], y_recv.at[k], (dp_to(c, 0), mp)))
        go(remote(w_rows(owner, dp), w_rows(owner, dp), c_send.at[rel], c_recv.at[rel], (dp_to(0, 1), mp)))

    def relay_z(a):
        rel = a * n_x
        await_w(rel)
        owner = mp_from(rel)
        for b in range(1, n_x):
            go(remote(w_rows(owner, dp), w_rows(owner, dp), w_send.at[rel + b], w_recv.at[rel + b], (dp, mp_to(b))))
        spread(rel)

    def relay_x(rel):
        await_w(rel)
        spread(rel)

    def relay_y(rel):
        owner = mp_from(rel)
        for c in range(1, n_y):
            k = c * n_mp + rel
            quarter = dp_from(c, 0)
            ref = w_rows(owner, quarter)
            remote(ref, ref, y_send.at[k], y_recv.at[k], (quarter, mp)).wait_recv()
            go(remote(ref, ref, c_send.at[k], c_recv.at[k], (dp_to(0, 1), mp)))

    own_codes.wait()
    users = codes_v.shape[0]
    home = home_ref[...]
    homes = home[:, :users]
    for k in range(1, n_dp):
        homes = jnp.where(dp == k, home[:, k * users:(k + 1) * users], homes)

    def code_part(target):
        base = (target * n_mp + mp) * slots
        wanted = base + lax.broadcasted_iota(jnp.int32, (slots, users), 0)
        pick = (homes == wanted).astype(F32).astype(BF16)
        return jnp.dot(pick, codes_v[...], preferred_element_type=F32)

    for c in range(n_y):
        for e in range(2):
            i = c * 2 + e
            code_parts[i] = code_part(dp_to(c, e))
            if i:
                go(remote(code_parts.at[i], code_recv.at[i], u_send.at[i], u_recv.at[i], (dp_to(c, e), mp)))

    own_table.wait()
    t_rows = table_v.shape[0]
    for i in range(t_rows // emb):
        block = table_v[pl.ds(i * emb, emb), :].astype(F32)
        table_t[:, pl.ds(i * emb, emb)] = block.T.astype(BF16)

    chunk = 512 if t_rows % 512 == 0 else t_rows

    def pool(target):
        picked = ids_ref[:, pl.ds(pl.multiple_of(target * rows, rows), rows)]
        total = jnp.zeros((emb, rows), F32)
        for i in range(t_rows // chunk):
            lanes = lax.broadcasted_iota(jnp.int32, (chunk, rows), 0) + i * chunk
            tally = jnp.zeros((chunk, rows), F32)
            for which in range(picked.shape[0]):
                tally = tally + jnp.where(lanes == picked[which:which + 1, :], 1.0, 0.0)
            total = total + jnp.dot(
                table_t[:, pl.ds(i * chunk, chunk)], tally.astype(BF16), preferred_element_type=F32
            )
        return total.T.astype(BF16)

    def columns(f):
        return pl.ds(pl.multiple_of(f * emb, emb), emb)

    def pool_send(low, high):
        def body(i, carry):
            rel = n_mp - 1 - i
            target = mp_to(rel)
            pooled[rel] = pool(target)
            remote(pooled.at[rel], x0.at[:, columns(mp)], p_send.at[rel], p_recv.at[rel], (dp, target)).start()
            return carry

        lax.fori_loop(low, high, body, 0)

    marks = [(n_mp - 1) * k // 7 for k in range(8)]
    for b in range(1, n_x):
        relay_x(b)
    pool_send(0, marks[1])
    for a in range(1, n_z):
        relay_z(a)
    pool_send(marks[1], marks[3])
    for b in range(1, n_x):
        for a in range(1, n_z):
            relay_x(a * n_x + b)
    pool_send(marks[3], marks[4])
    for b in range(1, n_x):
        relay_y(b)
    pool_send(marks[4], marks[5])
    relay_y(n_x)
    pool_send(marks[5], marks[6])
    for a in range(2, n_z):
        relay_y(a * n_x)
    pool_send(marks[6], n_mp - 1)
    x0[:, columns(mp)] = pool(mp)

    place = lax.broadcasted_iota(jnp.int32, (1, rows), 1)
    place_c = lax.broadcasted_iota(jnp.int32, (rows, 1), 0)
    seg = jnp.zeros((1, rows), jnp.int32)
    seg_c = jnp.zeros((rows, 1), jnp.int32)
    end = jnp.int32(0)
    for q in range(slots - 1):
        end = end + counts_ref[0, q]
        seg = seg + jnp.where(place >= end, 1, 0)
        seg_c = seg_c + jnp.where(place_c >= end, 1, 0)
    eye = place == place_c
    same = seg == seg_c
    labels = labels_ref[...]
    gain = jnp.ones((1, rows), F32)
    for level, step in ((1, 1.0), (2, 2.0), (3, 4.0), (4, 8.0)):
        gain = gain + jnp.where(labels >= level, step, 0.0)
    gain_c = jnp.sum(jnp.where(eye, gain, 0.0), axis=1, keepdims=True)
    norm = jnp.sum(jnp.where(same, gain - 1.0, 0.0), axis=1, keepdims=True)
    member = (seg_c == lax.broadcasted_iota(jnp.int32, (rows, slots), 1)).astype(F32).astype(BF16)

    for b in range(1, n_x):
        for a in range(1, n_z):
            relay_y(a * n_x + b)

    user_seg = code_parts[0]
    for i in range(1, n_dp):
        src = dp_from(i // 2, i % 2)
        remote(code_parts.at[i], code_recv.at[i], u_send.at[i], u_recv.at[i], (src, mp)).wait_recv()
        user_seg = user_seg + code_recv[i]
    user_seg = user_seg.astype(BF16)

    own_down.wait()
    own_up.wait()
    for rel in range(1, n_mp):
        src = mp_from(rel)
        remote(pooled.at[rel], x0.at[:, columns(src)], p_send.at[rel], p_recv.at[rel], (dp, src)).wait_recv()
    low = jnp.dot(x0[...], down[...], preferred_element_type=F32).astype(BF16)
    tile = 256

    def over(extent, body):
        step = tile if extent % tile == 0 else extent

        def run(i, carry):
            body(pl.ds(pl.multiple_of(i * step, step), step))
            return carry

        lax.fori_loop(0, extent // step, run, 0)

    def forward_cross(cols):
        lift = jnp.dot(low, up[:, cols], preferred_element_type=F32) + bias_ref[:, cols]
        own = x0[:, cols].astype(F32)
        cross[:, cols] = lift
        x1[:, cols] = (own * lift + own).astype(BF16)

    over(depth, forward_cross)

    own_w.wait()
    for rel in range(1, n_mp):
        owner = mp_from(rel)
        for c in range(n_y):
            k = c * n_mp + rel
            quarter = dp_from(c, 1)
            ref = w_rows(owner, quarter)
            remote(ref, ref, c_send.at[k], c_recv.at[k], (dp_to(0, 1), mp)).wait_recv()

    def forward_tower(cols):
        act[:, cols] = jnp.dot(x1[...], w_full[:, cols], preferred_element_type=F32) + tbias_ref[:, cols]

    over(width, forward_tower)
    scale = 1.0 / math.sqrt(width)
    value = act[...]
    sig = jax.nn.sigmoid(value)
    hidden = (value * sig).astype(BF16)
    code = jnp.dot(member, user_seg, preferred_element_type=F32)
    score_c = jnp.sum(hidden.astype(F32) * code, axis=1, keepdims=True) * scale
    score = jnp.sum(jnp.where(eye, score_c, 0.0), axis=0, keepdims=True)
    score_ref[...] = score

    diff = gain_c - gain
    gap = score - score_c
    turn = jax.nn.sigmoid(jnp.where(diff > 0, gap, -gap))
    total = jnp.sum(jnp.where(same, diff * turn, 0.0), axis=1, keepdims=True)
    dscore = -total / jnp.maximum(norm, 1.0)
    slope = sig * (1.0 + value * (1.0 - sig))
    dact = ((dscore * scale) * code * slope).astype(BF16)

    def backward_tower(cols):
        dx1[:, cols] = nt(dact, w_full[cols, :])

    over(depth, backward_tower)
    dcross = (dx1[...] * x0[...].astype(F32)).astype(BF16)
    dlow = nt(dcross, up[...]).astype(BF16)

    def grad(cols):
        flow = dx1[:, cols] * (1.0 + cross[:, cols]) + nt(dlow, down[cols, :])
        return flow.astype(BF16)

    def mine(f):
        return pl.ds(pl.multiple_of(f * rows, rows), rows)

    def grad_send(i, carry):
        rel = n_mp - 1 - i
        target = mp_to(rel)
        grads[rel] = grad(columns(target))
        remote(grads.at[rel], out_ref.at[mine(mp)], g_send.at[rel], g_recv.at[rel], (dp, target)).start()
        return carry

    lax.fori_loop(0, n_mp - 1, grad_send, 0)
    out_ref[mine(mp), :] = grad(columns(mp))

    for copy in sends:
        copy.wait_send()
    for rel in range(1, n_mp):
        target = mp_to(rel)
        src = mp_from(rel)
        remote(pooled.at[rel], x0.at[:, columns(mp)], p_send.at[rel], p_recv.at[rel], (dp, target)).wait_send()
        remote(grads.at[rel], out_ref.at[mine(mp)], g_send.at[rel], g_recv.at[rel], (dp, target)).wait_send()
        remote(grads.at[rel], out_ref.at[mine(src)], g_send.at[rel], g_recv.at[rel], (dp, src)).wait_recv()


def settle(score_in, grads_in, score_out, grads_out):
    score_out[...] = score_in[...]
    grads_out[...] = grads_in[...]


def local(n_dp, n_mp, table, ids, counts, labels, request_home, user_codes, cross_down, cross_up, cross_bias,
          tower_weight, tower_bias):
    n_x = max(d for d in range(1, math.isqrt(n_mp) + 1) if n_mp % d == 0)
    grid = (n_dp // 2, n_mp // n_x, n_x)
    rows = labels.shape[0]
    _, t_rows, emb = table.shape
    users, width = user_codes.shape
    depth, rank = cross_down.shape
    slots = counts.shape[1]
    everyone = rows * n_mp
    dma = pltpu.SemaphoreType.DMA
    hbm = pl.BlockSpec(memory_space=pltpu.HBM)
    vmem = pl.BlockSpec(memory_space=pltpu.VMEM)
    smem = pl.BlockSpec(memory_space=pltpu.SMEM)
    score, out = pl.pallas_call(
        functools.partial(kernel, grid),
        out_shape=(
            jax.ShapeDtypeStruct((1, rows), F32),
            jax.ShapeDtypeStruct((everyone, emb), BF16),
        ),
        in_specs=[hbm, vmem, smem, vmem, vmem, hbm, hbm, hbm, vmem, hbm, vmem],
        out_specs=(vmem, vmem),
        scratch_shapes=[
            pltpu.VMEM((t_rows, emb), BF16),
            pltpu.VMEM((emb, t_rows), BF16),
            pltpu.VMEM((users, width), BF16),
            pltpu.VMEM((depth, rank), BF16),
            pltpu.VMEM((rank, depth), BF16),
            pltpu.VMEM((depth, width), BF16),
            pltpu.VMEM((n_dp, slots, width), F32),
            pltpu.VMEM((n_dp, slots, width), F32),
            pltpu.VMEM((n_mp, rows, emb), BF16),
            pltpu.VMEM((rows, depth), BF16),
            pltpu.VMEM((rows, depth), BF16),
            pltpu.VMEM((rows, depth), F32),
            pltpu.VMEM((rows, width), F32),
            pltpu.VMEM((rows, depth), F32),
            pltpu.VMEM((n_mp, rows, emb), BF16),
            dma((5,)),
            dma((n_mp,)),
            dma((n_mp,)),
            dma((grid[0] * n_mp,)),
            dma((grid[0] * n_mp,)),
            dma((grid[0] * n_mp,)),
            dma((grid[0] * n_mp,)),
            dma((n_dp,)),
            dma((n_dp,)),
            dma((n_mp,)),
            dma((n_mp,)),
            dma((n_mp,)),
            dma((n_mp,)),
        ],
        compiler_params=pltpu.CompilerParams(
            collective_id=0, has_side_effects=True, vmem_limit_bytes=56 * 1024 * 1024
        ),
    )(
        table[0], ids[:, 0, :].T, counts, labels[None, :], request_home[None, :], user_codes,
        cross_down, cross_up, cross_bias[None, :], tower_weight, tower_bias[None, :],
    )
    score, out = pl.pallas_call(
        settle,
        out_shape=(
            jax.ShapeDtypeStruct((1, rows), F32),
            jax.ShapeDtypeStruct((everyone, emb), BF16),
        ),
        in_specs=[vmem, vmem],
        out_specs=(vmem, vmem),
        compiler_params=pltpu.CompilerParams(vmem_limit_bytes=56 * 1024 * 1024),
    )(score, out)
    return score[0], out[:, None, :]


def solution(mesh):
    in_specs = (
        P("mp", None, None),
        P("dp", "mp", None),
        P(("dp", "mp"), None),
        P(("dp", "mp")),
        P(),
        P("dp", None),
        P(),
        P(),
        P(),
        P("mp", None),
        P(),
    )
    out_specs = (P(("dp", "mp")), P("dp", "mp", None))
    body = functools.partial(local, mesh.shape["dp"], mesh.shape["mp"])
    return jax.shard_map(body, mesh=mesh, in_specs=in_specs, out_specs=out_specs, check_vma=False)
```
